32 devices in a mesh: dp: 2 (over core), row: 4 (over z), col: 4 (over y, x).
Axes of the slice: x: 2, y: 2, z: 4, core: 2. Of those that a mesh axis runs over, the one named last changes fastest.
Arguments:
- inputs: float32 [12000, 768], P(('dp', 'row', 'col')), may hold values from -6 to 6
- first_gain: float32 [768], replicated, may hold values from 0.25 to 1.75
- first_shift: float32 [768], replicated, may hold values from -3 to 3
- query_weight: bfloat16 [768, 768], P('row', 'col'), may hold values from -0.21875 to 0.21875
- query_bias: float32 [768], P('col'), may hold values from -2 to 2
- key_weight: bfloat16 [768, 768], P('row', 'col'), may hold values from -0.21875 to 0.21875
- value_weight: bfloat16 [768, 768], P('row', 'col'), may hold values from -0.21875 to 0.21875
- value_bias: float32 [768], P('col'), may hold values from -0.2 to 0.2
- out_weight: bfloat16 [768, 768], P('col', 'row'), may hold values from -4 to 4
- out_bias: float32 [768], replicated, may hold values from -2 to 2
- second_gain: float32 [768], replicated, may hold values from 0.25 to 1.75
- second_shift: float32 [768], replicated, may hold values from -3 to 3
- up_weight: bfloat16 [768, 3072], P('row', 'col'), may hold values from -0.21875 to 0.21875
- up_bias: float32 [3072], P('col'), may hold values from -3 to 3
- down_weight: bfloat16 [3072, 768], P('col', 'row'), may hold values from -0.21875 to 0.21875
- down_bias: float32 [768], replicated, may hold values from -2 to 2
- cotangent: float32 [12000, 768], P(('dp', 'row', 'col')), may hold values from -6 to 6
Outputs:
- result: float32 [12000, 768], P(('dp', 'row', 'col'))
- inputs_grad: float32 [12000, 768], P(('dp', 'row', 'col'))
- first_gain_grad: float32 [768], replicated
- first_shift_grad: float32 [768], replicated
- query_weight_grad: float32 [768, 768], P('row', 'col')
- query_bias_grad: float32 [768], P('col')
- key_weight_grad: float32 [768, 768], P('row', 'col')
- value_weight_grad: float32 [768, 768], P('row', 'col')
- value_bias_grad: float32 [768], P('col')
- out_weight_grad: float32 [768, 768], P('col', 'row')
- out_bias_grad: float32 [768], replicated
- second_gain_grad: float32 [768], replicated
- second_shift_grad: float32 [768], replicated
- up_weight_grad: float32 [768, 3072], P('row', 'col')
- up_bias_grad: float32 [3072], P('col')
- down_weight_grad: float32 [3072, 768], P('col', 'row')
- down_bias_grad: float32 [768], replicated
The draws below stay inside these ranges and needn't reach their ends.
All inputs are finite; a program needn't handle non-finite values.
Results may differ from the reference program's by a relative error of at most 0.011.
Values may be sent and summed in bfloat16 or wider, within the bound.
A program may use at most 192 MiB of HBM per device.

```python
import math
import jax
import jax.numpy as jnp
from jax import lax

D = 768
HEADS = 12
HEAD_DIM = 64
FF = 3072
LENGTH = 1500
TOKENS = 12000


def levels(rng, extent, split, low, high):
    gain, own = 1.0, jax.random.fold_in(rng, 6)
    for axis_at, shards_of in split:
        draws = jnp.exp(jax.random.uniform(jax.random.fold_in(own, axis_at), (shards_of,), jnp.float32, low / len(split), high / len(split)))
        gain = gain * jnp.repeat(draws, extent[axis_at] // shards_of).reshape([-1 if axis == axis_at else 1 for axis in range(len(extent))])
    return gain


def gaussian(stream_key, dims, deviation, most, pieces=(), dtype=jnp.bfloat16):
    array = jax.random.normal(stream_key, dims, jnp.float32) * deviation
    if len(pieces) > 0:
        array = levels(stream_key, dims, pieces, -0.22, 0.18) * array
    return jnp.clip(array, min=-most, max=most).astype(dtype)


def setup_inputs(seed: int = 0) -> dict:
    keys = jax.random.split(jax.random.key(seed), 18)
    inputs = gaussian(keys[0], (TOKENS, D), 1.0, 6.0, ((0, 32),), jnp.float32)
    first_gain = jnp.clip(1.0 + 0.15 * jax.random.normal(keys[1], (D,), jnp.float32), 0.25, 1.75)
    first_shift = gaussian(keys[2], (D,), 0.5, 3.0, (), jnp.float32)
    query_weight = gaussian(keys[3], (D, D), D ** -0.5, 0.21875, ((0, 4), (1, 4)))
    query_bias = gaussian(keys[4], (D,), 0.3, 2.0, ((0, 4),), jnp.float32)
    key_weight = gaussian(keys[5], (D, D), D ** -0.5, 0.21875, ((0, 4), (1, 4)))
    value_weight = gaussian(keys[6], (D, D), D ** -0.5, 0.21875, ((0, 4), (1, 4)))
    value_bias = gaussian(keys[7], (D,), 0.03, 0.2, ((0, 4),), jnp.float32)
    out_weight = gaussian(keys[8], (D, D), (max(1, D * 4 // LENGTH)) ** -0.5, 4.0, ((0, 4), (1, 4)))
    out_bias = gaussian(keys[9], (D,), 0.3, 2.0, (), jnp.float32)
    second_gain = jnp.clip(1.0 + 0.15 * jax.random.normal(keys[10], (D,), jnp.float32), 0.25, 1.75)
    second_shift = gaussian(keys[11], (D,), 0.5, 3.0, (), jnp.float32)
    up_weight = gaussian(keys[12], (D, FF), D ** -0.5, 0.21875, ((0, 4), (1, 4)))
    up_bias = gaussian(keys[13], (FF,), 0.5, 3.0, ((0, 4),), jnp.float32)
    down_weight = gaussian(keys[14], (FF, D), (FF // 4) ** -0.5, 0.21875, ((0, 4), (1, 4)))
    down_bias = gaussian(keys[15], (D,), 0.3, 2.0, (), jnp.float32)
    cotangent = gaussian(keys[16], (TOKENS, D), 1.0, 6.0, ((0, 32),), jnp.float32)
    return {"inputs": inputs, "first_gain": first_gain, "first_shift": first_shift, "query_weight": query_weight, "query_bias": query_bias, "key_weight": key_weight, "value_weight": value_weight, "value_bias": value_bias, "out_weight": out_weight, "out_bias": out_bias, "second_gain": second_gain, "second_shift": second_shift, "up_weight": up_weight, "up_bias": up_bias, "down_weight": down_weight, "down_bias": down_bias, "cotangent": cotangent}


@jax.custom_vjp
def low(v):
    return lax.optimization_barrier(v.astype(jnp.bfloat16)).astype(jnp.float32)

@jax.custom_vjp
def low_back(v):
    return v

def low_keep(v):
    return (low(v), None)

def low_pass(kept, grad):
    return (grad,)

def back_keep(v):
    return (v, None)

def back_low(kept, grad):
    return (low(grad),)
low.defvjp(low_keep, low_pass)
low_back.defvjp(back_keep, back_low)

def matmul(left_side, right_side):
    return jnp.dot(left_side, right_side, precision=lax.Precision.HIGHEST, preferred_element_type=jnp.float32)

def normalize(stream, scale_row, shift_row):
    center = lax.optimization_barrier(jnp.mean(stream, axis=1, keepdims=True))
    second = lax.optimization_barrier(jnp.mean(stream * stream, axis=1, keepdims=True))
    return (stream - center) * lax.rsqrt(second - center * center + 1e-05) * scale_row + shift_row

def clip_attention(bundle):
    query_rows, key_matrix_rows, value_rows = bundle
    softmax_scale = 1.0 / math.sqrt(HEAD_DIM)
    attention_scores = low_back(jnp.einsum('ugj,pgj->gup', query_rows, key_matrix_rows, precision=lax.Precision.HIGHEST) * softmax_scale)
    normalized_score_rows = low(jax.nn.softmax(attention_scores, axis=-1))
    return jnp.einsum('gqx,xgp->qgp', normalized_score_rows, value_rows, precision=lax.Precision.HIGHEST)

def encoder_layer(inputs, first_gain, first_shift, query_weight, query_bias, key_weight, value_weight, value_bias, out_weight, out_bias, second_gain, second_shift, up_weight, up_bias, down_weight, down_bias):
    attn_in = low(normalize(inputs, first_gain, first_shift))
    query_rows = low_back(low(matmul(attn_in, query_weight) + query_bias))
    key_matrix_rows = low_back(low(matmul(attn_in, key_weight)))
    value_rows = low_back(low(matmul(attn_in, value_weight) + value_bias))
    clip_shape = (TOKENS // LENGTH, LENGTH, HEADS, HEAD_DIM)
    attended_values = lax.map(jax.checkpoint(clip_attention), (query_rows.reshape(clip_shape), key_matrix_rows.reshape(clip_shape), value_rows.reshape(clip_shape)))
    attended_values = low_back(low(attended_values.reshape(TOKENS, D)))
    middle = inputs + low_back(matmul(attended_values, out_weight) + out_bias)
    mlp_in = low(normalize(middle, second_gain, second_shift))
    pre_act = low_back(matmul(mlp_in, up_weight) + up_bias)
    hidden = low(jax.nn.gelu(pre_act, approximate=False))
    return middle + low_back(matmul(hidden, down_weight) + down_bias)

def reference(inputs, first_gain, first_shift, query_weight, query_bias, key_weight, value_weight, value_bias, out_weight, out_bias, second_gain, second_shift, up_weight, up_bias, down_weight, down_bias, cotangent):
    floats = (inputs, first_gain, first_shift, query_weight.astype(jnp.float32), query_bias, key_weight.astype(jnp.float32), value_weight.astype(jnp.float32), value_bias, out_weight.astype(jnp.float32), out_bias, second_gain, second_shift, up_weight.astype(jnp.float32), up_bias, down_weight.astype(jnp.float32), down_bias)
    result, pullback = jax.vjp(encoder_layer, *floats)
    gradients = pullback(cotangent)
    return (result, gradients[0], gradients[1], gradients[2], gradients[3], gradients[4], gradients[5], gradients[6], gradients[7], gradients[8], gradients[9], gradients[10], gradients[11], gradients[12], gradients[13], gradients[14], gradients[15])
```

```python
import functools

import jax
import jax.numpy as jnp
from jax import lax
from jax.experimental import pallas as pl
from jax.experimental.pallas import tpu as pltpu
from jax.sharding import PartitionSpec as P

HEAD_DIM = 64
LENGTH = 1500
LOG2E = 1.4426950408889634
SCALE = HEAD_DIM**-0.5
BLOCK = 256
F32 = jnp.float32
BF16 = jnp.bfloat16


def dims(left_dim, right_dim):
    return (((left_dim,), (right_dim,)), ((), ()))


def dot(left_side, right_side, left_dim, right_dim):
    return lax.dot_general(
        left_side, right_side, dims(left_dim, right_dim), preferred_element_type=F32
    )


def norm_stats(stream):
    center = jnp.mean(stream, axis=1, keepdims=True)
    second = jnp.mean(stream * stream, axis=1, keepdims=True)
    inverse = lax.rsqrt(second - center * center + 1e-05)
    return (stream - center) * inverse, inverse


def norm_backward(upstream, normed, inverse, scale_row):
    scaled = upstream * scale_row
    back_rows = inverse * (
        scaled
        - jnp.mean(scaled, axis=1, keepdims=True)
        - normed * jnp.mean(scaled * normed, axis=1, keepdims=True)
    )
    return back_rows, jnp.sum(upstream * normed, axis=0), jnp.sum(upstream, axis=0)


def key_bias(keys, block_rows, real_rows):
    at = lax.broadcasted_iota(jnp.int32, (keys, 1), 0)
    return jnp.where(lax.rem(at, block_rows) < real_rows, 0.0, -1e30).astype(F32)


def forward_kernel(heads, block_rows, real_rows, q_ref, k_ref, v_ref, o_ref, lse_ref):
    bias = key_bias(k_ref.shape[0], block_rows, real_rows)
    for head in range(heads):
        cols = slice(head * HEAD_DIM, (head + 1) * HEAD_DIM)
        queries, keys, values = q_ref[:, cols], k_ref[:, cols], v_ref[:, cols]
        scores = dot(keys, queries, 1, 1) * (SCALE * LOG2E) + bias
        highest = jnp.max(scores, axis=0, keepdims=True)
        exponent = jnp.exp2(scores - highest)
        summed = jnp.sum(exponent, axis=0, keepdims=True)
        probs = (exponent * (1.0 / summed)).astype(BF16)
        turned = dot(values, probs, 0, 0)
        o_ref[:, cols] = jnp.transpose(turned).astype(BF16)
        lse_ref[head : head + 1, :] = highest + jnp.log2(summed)


def backward_kernel(
    heads, block_rows, real_rows,
    q_ref, k_ref, v_ref, g_ref, lse_ref, dq_ref, dk_ref, dv_ref, dk_sum, dv_sum,
):
    step = pl.program_id(0)

    @pl.when(step == 0)
    def _():
        dk_sum[...] = jnp.zeros_like(dk_sum)
        dv_sum[...] = jnp.zeros_like(dv_sum)

    bias = key_bias(k_ref.shape[0], block_rows, real_rows)
    for head in range(heads):
        cols = slice(head * HEAD_DIM, (head + 1) * HEAD_DIM)
        queries, keys, values = q_ref[:, cols], k_ref[:, cols], v_ref[:, cols]
        grads = g_ref[:, cols]
        scores = dot(keys, queries, 1, 1) * (SCALE * LOG2E) + bias
        probs = jnp.exp2(scores - lse_ref[head : head + 1, :])
        prob_grad = dot(values, grads, 1, 1)
        inner = jnp.sum(probs * prob_grad, axis=0, keepdims=True)
        score_grad = (probs * (prob_grad - inner)).astype(BF16)
        dv_sum[head] += dot(probs.astype(BF16), grads, 1, 0)
        dk_sum[head] += dot(score_grad, queries, 1, 0)
        turned = dot(keys, score_grad, 0, 0)
        dq_ref[:, cols] = (jnp.transpose(turned) * SCALE).astype(BF16)

    @pl.when(step == pl.num_programs(0) - 1)
    def _():
        for head in range(heads):
            cols = slice(head * HEAD_DIM, (head + 1) * HEAD_DIM)
            dk_ref[:, cols] = (dk_sum[head] * SCALE).astype(BF16)
            dv_ref[:, cols] = dv_sum[head].astype(BF16)


def attention_forward(q, k, v, block_rows, real_rows):
    tokens, width = q.shape
    heads = width // HEAD_DIM
    part = pl.BlockSpec((BLOCK, width), lambda i: (i, 0))
    whole = pl.BlockSpec((tokens, width), lambda i: (0, 0))
    return pl.pallas_call(
        functools.partial(forward_kernel, heads, block_rows, real_rows),
        grid=(tokens // BLOCK,),
        in_specs=[part, whole, whole],
        out_specs=[part, pl.BlockSpec((8, BLOCK), lambda i: (0, i))],
        out_shape=[
            jax.ShapeDtypeStruct((tokens, width), BF16),
            jax.ShapeDtypeStruct((8, tokens), F32),
        ],
        compiler_params=pltpu.CompilerParams(vmem_limit_bytes=40 * 1024 * 1024),
        cost_estimate=pl.CostEstimate(
            flops=16 * tokens * tokens * width,
            bytes_accessed=8 * tokens * width,
            transcendentals=heads * tokens * tokens,
        ),
        name="attention_forward",
    )(q, k, v)


def attention_backward(q, k, v, grads, lse, block_rows, real_rows):
    tokens, width = q.shape
    heads = width // HEAD_DIM
    part = pl.BlockSpec((BLOCK, width), lambda i: (i, 0))
    whole = pl.BlockSpec((tokens, width), lambda i: (0, 0))
    shape = jax.ShapeDtypeStruct((tokens, width), BF16)
    return pl.pallas_call(
        functools.partial(backward_kernel, heads, block_rows, real_rows),
        grid=(tokens // BLOCK,),
        in_specs=[part, whole, whole, part, pl.BlockSpec((8, BLOCK), lambda i: (0, i))],
        out_specs=[part, whole, whole],
        out_shape=[shape, shape, shape],
        scratch_shapes=[
            pltpu.VMEM((heads, tokens, HEAD_DIM), F32),
            pltpu.VMEM((heads, tokens, HEAD_DIM), F32),
        ],
        compiler_params=pltpu.CompilerParams(vmem_limit_bytes=40 * 1024 * 1024),
        cost_estimate=pl.CostEstimate(
            flops=40 * tokens * tokens * width,
            bytes_accessed=14 * tokens * width,
            transcendentals=heads * tokens * tokens,
        ),
        name="attention_backward",
    )(q, k, v, grads, lse)


def swap(block, axis, size, step):
    return lax.ppermute(block, axis, [(i, i ^ step) for i in range(size)])


def few(size):
    return size <= 8 and size & (size - 1) == 0


def tree(terms):
    while len(terms) > 1:
        terms = [terms[i] + terms[i + 1] for i in range(0, len(terms), 2)]
    return terms[0]


def spread(block, axis, size):
    return [block] + [swap(block, axis, size, j) for j in range(1, size)]


def exchange(blocks, axis, size):
    return [blocks[0]] + [swap(blocks[j], axis, size, j) for j in range(1, size)]


def sum_blocks(make, axis, size):
    sent = {j: swap(make(j).astype(BF16), axis, size, j) for j in reversed(range(1, size))}
    return tree([make(0)] + [sent[j].astype(F32) for j in range(1, size)])


def sum_all(vector, axis, size):
    if few(size):
        return tree(spread(vector, axis, size))
    return lax.psum(vector, axis)


def sum_weight(part, rows, dps):
    depth, width = part.shape
    if dps != 2:
        own = lax.psum_scatter(part, "row", scatter_dimension=0, tiled=True)
        return lax.psum(own, "dp")
    half = depth // rows // 2
    first = lax.axis_index("dp") == 0
    view = part.reshape(rows, 2, half, width)
    mine = jnp.where(first, view[:, 0], view[:, 1])
    other = jnp.where(first, view[:, 1], view[:, 0]).astype(BF16)
    total = mine + swap(other, "dp", 2, 1).astype(F32)
    if few(rows):
        me = lax.axis_index("row")
        pick = lambda j: lax.dynamic_index_in_dim(total, jnp.bitwise_xor(me, j), 0, False)
        total = sum_blocks(pick, "row", rows)
    else:
        total = lax.psum_scatter(total, "row", scatter_dimension=0, tiled=True)[0]
    theirs = swap(total, "dp", 2, 1)
    return jnp.where(
        first,
        jnp.concatenate([total, theirs], axis=0),
        jnp.concatenate([theirs, total], axis=0),
    )


def per_device(
    cols, rows, dps,
    inputs, first_gain, first_shift, query_weight, query_bias, key_weight, value_weight,
    value_bias, out_weight, out_bias, second_gain, second_shift, up_weight, up_bias,
    down_weight, down_bias, cotangent,
):
    real = inputs.shape[0]
    held = -(-real // 128) * 128
    width = inputs.shape[1]
    head_cols = query_weight.shape[1]
    assert real * cols == LENGTH and cols & (cols - 1) == 0
    fill = ((0, held - real), (0, 0))
    padded = jnp.pad(inputs, fill)
    cotangent = jnp.pad(cotangent, fill)

    def block(array, j):
        return array[j * held : (j + 1) * held]

    def join(blocks):
        return jnp.concatenate(blocks, axis=0)

    joined = lax.all_gather(
        jnp.concatenate([query_weight, key_weight, value_weight], axis=1), "row", axis=0, tiled=True
    )
    rest = lax.all_gather(
        jnp.concatenate([out_weight.T, up_weight, down_weight.T], axis=1), "row", axis=0, tiled=True
    )
    out_turned = rest[:, :head_cols]
    hidden_cols = up_weight.shape[1]
    up_full = rest[:, head_cols : head_cols + hidden_cols]
    down_turned = rest[:, head_cols + hidden_cols :]

    first_normed, first_inverse = norm_stats(padded)
    attn_in = (first_normed * first_gain + first_shift).astype(BF16)
    attn_all = join(spread(attn_in, "col", cols))
    projected = dot(attn_all, joined, 1, 0)
    queries = (projected[:, :head_cols] + query_bias).astype(BF16)
    keys = projected[:, head_cols : 2 * head_cols].astype(BF16)
    values = (projected[:, 2 * head_cols :] + value_bias).astype(BF16)

    out_full = jnp.concatenate(spread(out_turned, "col", cols), axis=1)
    out_grad = cotangent.astype(BF16)
    out_all = join(spread(out_grad, "col", cols))

    attended, lse = attention_forward(queries, keys, values, held, real)
    attended_own = jnp.concatenate(
        exchange([block(attended, j) for j in range(cols)], "col", cols), axis=1
    )
    middle = padded + (dot(attended_own, out_full, 1, 1) + out_bias)
    second_normed, second_inverse = norm_stats(middle)
    mlp_in = (second_normed * second_gain + second_shift).astype(BF16)
    mlp_all = join(spread(mlp_in, "col", cols))
    pre_act = dot(mlp_all, up_full, 1, 0) + up_bias
    hidden_grad = dot(out_all, down_turned, 1, 0)
    below = 0.5 * (1.0 + lax.erf(pre_act * (0.5**0.5)))
    slope = below + pre_act * (jnp.exp(-0.5 * pre_act * pre_act) * 0.3989422804014327)
    hidden = (pre_act * below).astype(BF16)
    pre_grad = (hidden_grad * slope).astype(BF16)
    mlp_back = sum_blocks(lambda j: dot(block(pre_grad, j), up_full, 1, 1), "col", cols)
    norm_rows, second_gain_part, second_shift_part = norm_backward(
        mlp_back, second_normed, second_inverse, second_gain
    )
    middle_grad = cotangent + norm_rows
    attn_grad = middle_grad.astype(BF16)
    attended_grad_own = dot(attn_grad, out_full, 1, 0).astype(BF16)
    attended_grad = join(
        exchange(
            [attended_grad_own[:, j * head_cols : (j + 1) * head_cols] for j in range(cols)],
            "col",
            cols,
        )
    )
    query_grad, key_grad, value_grad = attention_backward(
        queries, keys, values, attended_grad, lse, held, real
    )

    hidden_late, _ = lax.optimization_barrier((hidden, mlp_back))
    result = middle + (
        sum_blocks(lambda j: dot(block(hidden_late, j), down_turned, 1, 1), "col", cols) + down_bias
    )
    up_part = dot(mlp_all, pre_grad, 0, 0)
    down_part = dot(out_all, hidden, 0, 0)
    mlp_sum = sum_weight(jnp.concatenate([up_part, down_part], axis=1), rows, dps)
    out_part = sum_blocks(
        lambda j: dot(attn_grad, attended_own[:, j * head_cols : (j + 1) * head_cols], 0, 0),
        "col",
        cols,
    )
    out_sum = sum_weight(out_part, rows, dps)
    up_bias_part = jnp.sum(pre_grad, axis=0, dtype=F32)
    early = jnp.concatenate([
        second_gain_part,
        second_shift_part,
        jnp.sum(attn_grad, axis=0, dtype=F32),
        jnp.sum(out_grad, axis=0, dtype=F32),
    ])
    early = jnp.concatenate([sum_all(early, "col", cols), up_bias_part])
    early = sum_all(sum_all(early, "row", rows), "dp", dps)

    grad_rows = jnp.concatenate([query_grad, key_grad, value_grad], axis=1)
    attn_back = sum_blocks(lambda j: dot(block(grad_rows, j), joined, 1, 1), "col", cols)
    qkv_sum = sum_weight(dot(attn_all, grad_rows, 0, 0), rows, dps)
    norm_rows, first_gain_part, first_shift_part = norm_backward(
        attn_back, first_normed, first_inverse, first_gain
    )
    inputs_grad = middle_grad + norm_rows
    late = sum_all(jnp.concatenate([first_gain_part, first_shift_part]), "col", cols)
    late = jnp.concatenate([
        late,
        jnp.sum(query_grad, axis=0, dtype=F32),
        jnp.sum(value_grad, axis=0, dtype=F32),
    ])
    late = sum_all(sum_all(late, "row", rows), "dp", dps)

    return (
        result[:real],
        inputs_grad[:real],
        late[:width],
        late[width : 2 * width],
        qkv_sum[:, :head_cols],
        late[2 * width : 2 * width + head_cols],
        qkv_sum[:, head_cols : 2 * head_cols],
        qkv_sum[:, 2 * head_cols :],
        late[2 * width + head_cols :],
        out_sum.T,
        early[2 * width : 3 * width],
        early[:width],
        early[width : 2 * width],
        mlp_sum[:, :hidden_cols],
        early[4 * width :],
        mlp_sum[:, hidden_cols:].T,
        early[3 * width : 4 * width],
    )


def solution(mesh):
    stream = P(("dp", "row", "col"), None)
    inward, outward = P("row", "col"), P("col", "row")
    return jax.shard_map(
        functools.partial(
            per_device, mesh.shape["col"], mesh.shape["row"], mesh.shape["dp"]
        ),
        mesh=mesh,
        in_specs=(
            stream, P(), P(), inward, P("col"), inward, inward, P("col"), outward, P(), P(), P(),
            inward, P("col"), outward, P(), stream,
        ),
        out_specs=(
            stream, stream, P(), P(), inward, P("col"), inward, inward, P("col"), outward, P(),
            P(), P(), inward, P("col"), outward, P(),
        ),
        check_vma=False,
    )
```

```python
import functools

import jax
import jax.numpy as jnp
from jax import lax
from jax.experimental import pallas as pl
from jax.experimental.pallas import tpu as pltpu
from jax.sharding import PartitionSpec as P

HEAD_DIM = 64
LENGTH = 1500
LOG2E = 1.4426950408889634
SCALE = HEAD_DIM**-0.5
BLOCK = 256
F32 = jnp.float32
BF16 = jnp.bfloat16


def dims(left_dim, right_dim):
    return (((left_dim,), (right_dim,)), ((), ()))


def dot(left_side, right_side, left_dim, right_dim):
    return lax.dot_general(
        left_side, right_side, dims(left_dim, right_dim), preferred_element_type=F32
    )


def norm_stats(stream):
    center = jnp.mean(stream, axis=1, keepdims=True)
    second = jnp.mean(stream * stream, axis=1, keepdims=True)
    inverse = lax.rsqrt(second - center * center + 1e-05)
    return (stream - center) * inverse, inverse


def norm_backward(upstream, normed, inverse, scale_row):
    scaled = upstream * scale_row
    back_rows = inverse * (
        scaled
        - jnp.mean(scaled, axis=1, keepdims=True)
        - normed * jnp.mean(scaled * normed, axis=1, keepdims=True)
    )
    return back_rows, jnp.sum(upstream * normed, axis=0), jnp.sum(upstream, axis=0)


def key_bias(keys, block_rows, real_rows):
    at = lax.broadcasted_iota(jnp.int32, (keys, 1), 0)
    return jnp.where(lax.rem(at, block_rows) < real_rows, 0.0, -1e30).astype(F32)


def head_at(kind, heads, head):
    start = (kind * heads + head) * HEAD_DIM
    return slice(start, start + HEAD_DIM)


def forward_kernel(heads, block_rows, real_rows, part_ref, whole_ref, o_ref, lse_ref):
    bias = key_bias(whole_ref.shape[0], block_rows, real_rows)
    for head in range(heads):
        queries = part_ref[:, head_at(0, heads, head)]
        keys = whole_ref[:, head_at(1, heads, head)]
        values = whole_ref[:, head_at(2, heads, head)]
        scores = dot(keys, queries, 1, 1) * (SCALE * LOG2E) + bias
        highest = jnp.max(scores, axis=0, keepdims=True)
        exponent = jnp.exp2(scores - highest)
        summed = jnp.sum(exponent, axis=0, keepdims=True)
        probs = (exponent * (1.0 / summed)).astype(BF16)
        turned = dot(values, probs, 0, 0)
        o_ref[:, head_at(0, heads, head)] = jnp.transpose(turned).astype(BF16)
        lse_ref[head : head + 1, :] = highest + jnp.log2(summed)


def backward_kernel(
    heads, block_rows, real_rows, part_ref, whole_ref, g_ref, lse_ref, out_ref, dk_sum, dv_sum
):
    step = pl.program_id(0)

    @pl.when(step == 0)
    def _():
        dk_sum[...] = jnp.zeros_like(dk_sum)
        dv_sum[...] = jnp.zeros_like(dv_sum)

    bias = key_bias(whole_ref.shape[0], block_rows, real_rows)
    at = pl.ds(pl.multiple_of(step * BLOCK, BLOCK), BLOCK)
    for head in range(heads):
        queries = part_ref[:, head_at(0, heads, head)]
        keys = whole_ref[:, head_at(1, heads, head)]
        values = whole_ref[:, head_at(2, heads, head)]
        grads = g_ref[:, head_at(0, heads, head)]
        scores = dot(keys, queries, 1, 1) * (SCALE * LOG2E) + bias
        probs = jnp.exp2(scores - lse_ref[head : head + 1, :])
        prob_grad = dot(values, grads, 1, 1)
        inner = jnp.sum(probs * prob_grad, axis=0, keepdims=True)
        score_grad = (probs * (prob_grad - inner)).astype(BF16)
        dv_sum[head] += dot(probs.astype(BF16), grads, 1, 0)
        dk_sum[head] += dot(score_grad, queries, 1, 0)
        turned = dot(keys, score_grad, 0, 0)
        out_ref[at, head_at(0, heads, head)] = (jnp.transpose(turned) * SCALE).astype(BF16)

    @pl.when(step == pl.num_programs(0) - 1)
    def _():
        for head in range(heads):
            out_ref[:, head_at(1, heads, head)] = (dk_sum[head] * SCALE).astype(BF16)
            out_ref[:, head_at(2, heads, head)] = dv_sum[head].astype(BF16)


def attention_forward(qkv, first, count, block_rows, real_rows):
    tokens, width = qkv.shape[0], qkv.shape[1] // 3
    heads = width // HEAD_DIM
    start = first // BLOCK
    return pl.pallas_call(
        functools.partial(forward_kernel, heads, block_rows, real_rows),
        grid=(count // BLOCK,),
        in_specs=[
            pl.BlockSpec((BLOCK, 3 * width), lambda i: (i + start, 0)),
            pl.BlockSpec((tokens, 3 * width), lambda i: (0, 0)),
        ],
        out_specs=[
            pl.BlockSpec((BLOCK, width), lambda i: (i, 0)),
            pl.BlockSpec((8, BLOCK), lambda i: (0, i)),
        ],
        out_shape=[
            jax.ShapeDtypeStruct((count, width), BF16),
            jax.ShapeDtypeStruct((8, count), F32),
        ],
        compiler_params=pltpu.CompilerParams(vmem_limit_bytes=40 * 1024 * 1024),
        cost_estimate=pl.CostEstimate(
            flops=16 * count * tokens * width,
            bytes_accessed=8 * tokens * width,
            transcendentals=heads * count * tokens,
        ),
        name="attention_forward",
    )(qkv, qkv)


def attention_backward(qkv, grads, lse, block_rows, real_rows):
    tokens, width = grads.shape
    heads = width // HEAD_DIM
    whole = pl.BlockSpec((tokens, 3 * width), lambda i: (0, 0))
    return pl.pallas_call(
        functools.partial(backward_kernel, heads, block_rows, real_rows),
        grid=(tokens // BLOCK,),
        in_specs=[
            pl.BlockSpec((BLOCK, 3 * width), lambda i: (i, 0)),
            whole,
            pl.BlockSpec((BLOCK, width), lambda i: (i, 0)),
            pl.BlockSpec((8, BLOCK), lambda i: (0, i)),
        ],
        out_specs=whole,
        out_shape=jax.ShapeDtypeStruct((tokens, 3 * width), BF16),
        scratch_shapes=[
            pltpu.VMEM((heads, tokens, HEAD_DIM), F32),
            pltpu.VMEM((heads, tokens, HEAD_DIM), F32),
        ],
        compiler_params=pltpu.CompilerParams(vmem_limit_bytes=40 * 1024 * 1024),
        cost_estimate=pl.CostEstimate(
            flops=40 * tokens * tokens * width,
            bytes_accessed=14 * tokens * width,
            transcendentals=heads * tokens * tokens,
        ),
        name="attention_backward",
    )(qkv, qkv, grads, lse)


def swap(block, axis, size, step):
    return lax.ppermute(block, axis, [(i, i ^ step) for i in range(size)])


def few(size):
    return size <= 8 and size & (size - 1) == 0


def tree(terms):
    while len(terms) > 1:
        terms = [terms[i] + terms[i + 1] for i in range(0, len(terms), 2)]
    return terms[0]


def spread(block, axis, size):
    return [block] + [swap(block, axis, size, j) for j in range(1, size)]


def exchange(blocks, axis, size):
    return [blocks[0]] + [swap(blocks[j], axis, size, j) for j in range(1, size)]


def gather_rows(block, axis, size):
    if size != 4:
        return jnp.concatenate(spread(block, axis, size), axis=0)
    half = block.shape[1] // 2
    one = swap(block, axis, size, 1)
    two = swap(block, axis, size, 2)
    left = swap(one[:, :half], axis, size, 2)
    right = swap(two[:, half:], axis, size, 1)
    return jnp.concatenate([block, one, two, jnp.concatenate([left, right], axis=1)], axis=0)


def sum_blocks(make, axis, size):
    sent = {j: swap(make(j).astype(BF16), axis, size, j) for j in reversed(range(1, size))}
    return tree([make(0)] + [sent[j].astype(F32) for j in range(1, size)])


def send_products(source, weight, held, axis, size):
    rows = lambda j: source[j * held : (j + 1) * held]
    if size != 4:
        return [swap(dot(rows(j), weight, 1, 1).astype(BF16), axis, size, j) for j in range(1, size)]
    half = weight.shape[0] // 2
    pair = jnp.concatenate([rows(1), rows(3)], axis=0)
    one = swap(dot(pair, weight[:half], 1, 1).astype(BF16), axis, size, 1)
    two = swap(dot(source[2 * held :], weight[half:], 1, 1).astype(BF16), axis, size, 2)
    return [one, two]


def add_products(found, source, weight, held, axis, size):
    rows = lambda j: source[j * held : (j + 1) * held]
    own = dot(rows(0), weight, 1, 1)
    if size != 4:
        return tree([own] + [term.astype(F32) for term in found])
    half = weight.shape[0] // 2
    one, two = found
    far_left = dot(rows(2), weight[:half], 1, 1) + one[held:].astype(F32)
    far_right = dot(rows(1), weight[half:], 1, 1) + two[held:].astype(F32)
    left_back = swap(far_left.astype(BF16), axis, size, 2)
    right_back = swap(far_right.astype(BF16), axis, size, 1)
    near = jnp.concatenate([one[:held], two[:held]], axis=1).astype(F32)
    back = jnp.concatenate([left_back, right_back], axis=1).astype(F32)
    return own + near + back


def sum_products(source, weight, held, axis, size):
    found = send_products(source, weight, held, axis, size)
    return add_products(found, source, weight, held, axis, size)


def sum_all(vector, axis, size):
    if few(size):
        return tree(spread(vector, axis, size))
    return lax.psum(vector, axis)


def gather_weight(block, rows, dps, offload):
    if dps != 2:
        return lax.all_gather(block, "row", axis=0, tiled=True)
    half = block.shape[0] // 2
    first = lax.axis_index("dp") == 0
    mine = jnp.where(first, block[:half], block[half:])
    if offload or not few(rows):
        return lax.all_gather(mine, ("row", "dp"), axis=0, tiled=True)
    me = lax.axis_index("row")
    found = jnp.stack(spread(mine, "row", rows))
    order = [
        lax.dynamic_index_in_dim(found, jnp.bitwise_xor(me, r), 0, False) for r in range(rows)
    ]
    mine = jnp.stack(order)
    theirs = swap(mine, "dp", 2, 1)
    whole = jnp.stack([jnp.where(first, mine, theirs), jnp.where(first, theirs, mine)], axis=1)
    return whole.reshape(2 * half * rows, block.shape[1])


def halve_weight(part, rows, dps):
    depth, width = part.shape
    half = depth // rows // dps
    first = lax.axis_index("dp") == 0
    view = part.reshape(rows, dps, half, width)
    mine = jnp.where(first, view[:, 0], view[:, 1])
    other = jnp.where(first, view[:, 1], view[:, 0]).astype(BF16)
    return mine + swap(other, "dp", dps, 1).astype(F32)


def sum_weight(total, rows):
    if few(rows):
        me = lax.axis_index("row")
        pick = lambda j: lax.dynamic_index_in_dim(total, jnp.bitwise_xor(me, j), 0, False)
        return sum_blocks(pick, "row", rows)
    return lax.psum_scatter(total, "row", scatter_dimension=0, tiled=True)[0]


def rejoin_weight(total, dps):
    first = lax.axis_index("dp") == 0
    theirs = swap(total, "dp", dps, 1)
    return jnp.where(
        first,
        jnp.concatenate([total, theirs], axis=0),
        jnp.concatenate([theirs, total], axis=0),
    )


def per_device(
    cols, rows, dps,
    inputs, first_gain, first_shift, query_weight, query_bias, key_weight, value_weight,
    value_bias, out_weight, out_bias, second_gain, second_shift, up_weight, up_bias,
    down_weight, down_bias, cotangent,
):
    real = inputs.shape[0]
    held = -(-real // 128) * 128
    width = inputs.shape[1]
    head_cols = query_weight.shape[1]
    assert real * cols == LENGTH and cols & (cols - 1) == 0
    fill = ((0, held - real), (0, 0))
    padded = jnp.pad(inputs, fill)
    cotangent = jnp.pad(cotangent, fill)

    def block(array, j):
        return array[j * held : (j + 1) * held]

    def join(blocks):
        return jnp.concatenate(blocks, axis=0)

    assert dps == 2
    first_normed, first_inverse = norm_stats(padded)
    attn_in = (first_normed * first_gain + first_shift).astype(BF16)
    near = gather_weight(
        jnp.concatenate([query_weight, key_weight, value_weight, out_weight.T], axis=1),
        rows, dps, False,
    )
    joined, out_turned = near[:, : 3 * head_cols], near[:, 3 * head_cols :]
    attn_all = gather_rows(attn_in, "col", cols)
    rest = gather_weight(jnp.concatenate([up_weight, down_weight.T], axis=1), rows, dps, True)
    hidden_cols = up_weight.shape[1]
    up_full, down_turned = rest[:, :hidden_cols], rest[:, hidden_cols:]

    joined_bias = jnp.concatenate([query_bias, jnp.zeros_like(query_bias), value_bias])
    qkv = (dot(attn_all, joined, 1, 0) + joined_bias).astype(BF16)

    out_grad = cotangent.astype(BF16)
    out_all = gather_rows(out_grad, "col", cols)
    out_full = jnp.concatenate(spread(out_turned, "col", cols), axis=1)
    middle_at = cols // 2 * held
    attended_far, lse_far = attention_forward(
        qkv, middle_at, cols * held - middle_at, held, real
    )
    qkv, out_all, out_full, up_full, down_turned = lax.optimization_barrier(
        (qkv, out_all, out_full, up_full, down_turned)
    )
    attended_near, lse_near = attention_forward(qkv, 0, middle_at, held, real)
    halves = [block(attended_near, j) for j in range(cols // 2)]
    halves += [block(attended_far, j) for j in range(cols - cols // 2)]
    attended_own = jnp.concatenate(exchange(halves, "col", cols), axis=1)
    lse = jnp.concatenate([lse_near, lse_far], axis=1)

    middle = padded + (dot(attended_own, out_full, 1, 1) + out_bias)
    second_normed, second_inverse = norm_stats(middle)
    mlp_in = (second_normed * second_gain + second_shift).astype(BF16)
    mlp_all = gather_rows(mlp_in, "col", cols)
    pre_act = dot(mlp_all, up_full, 1, 0) + up_bias
    hidden_grad = dot(out_all, down_turned, 1, 0)
    below = 0.5 * (1.0 + lax.erf(pre_act * (0.5**0.5)))
    slope = below + pre_act * (jnp.exp(-0.5 * pre_act * pre_act) * 0.3989422804014327)
    hidden = (pre_act * below).astype(BF16)
    pre_grad = (hidden_grad * slope).astype(BF16)
    mlp_back = sum_products(pre_grad, up_full, held, "col", cols)
    up_part = dot(mlp_all, pre_grad, 0, 0)
    down_part = dot(out_all, hidden, 0, 0)
    mlp_half = halve_weight(jnp.concatenate([up_part, down_part], axis=1), rows, dps)
    up_bias_part = jnp.sum(pre_grad, axis=0, dtype=F32)
    norm_rows, second_gain_part, second_shift_part = norm_backward(
        mlp_back, second_normed, second_inverse, second_gain
    )
    middle_grad = cotangent + norm_rows
    attn_grad = middle_grad.astype(BF16)
    attended_grad_own = dot(attn_grad, out_full, 1, 0).astype(BF16)
    attended_grad = join(
        exchange(
            [attended_grad_own[:, j * head_cols : (j + 1) * head_cols] for j in range(cols)],
            "col",
            cols,
        )
    )

    attended_grad, hidden_late, mlp_half, attn_late = lax.optimization_barrier(
        (attended_grad, hidden, mlp_half, attn_grad)
    )
    down_found = send_products(hidden_late, down_turned, held, "col", cols)
    mlp_sum = sum_weight(mlp_half, rows)
    out_part = sum_blocks(
        lambda j: dot(attn_late, attended_own[:, j * head_cols : (j + 1) * head_cols], 0, 0),
        "col",
        cols,
    )
    grad_rows = attention_backward(qkv, attended_grad, lse, held, real)
    grad_rows, down_found, mlp_sum = lax.optimization_barrier((grad_rows, down_found, mlp_sum))
    down_sum = add_products(down_found, hidden_late, down_turned, held, "col", cols)
    result = middle + (down_sum + down_bias)

    attn_back = sum_products(grad_rows, joined, held, "col", cols)
    near_part = jnp.concatenate([dot(attn_all, grad_rows, 0, 0), out_part], axis=1)
    near_sum = rejoin_weight(sum_weight(halve_weight(near_part, rows, dps), rows), dps)
    mlp_sum = rejoin_weight(mlp_sum, dps)
    qkv_sum, out_sum = near_sum[:, : 3 * head_cols], near_sum[:, 3 * head_cols :]
    norm_rows, first_gain_part, first_shift_part = norm_backward(
        attn_back, first_normed, first_inverse, first_gain
    )
    inputs_grad = middle_grad + norm_rows
    vector = jnp.concatenate([
        first_gain_part,
        first_shift_part,
        second_gain_part,
        second_shift_part,
        jnp.sum(attn_grad, axis=0, dtype=F32),
        jnp.sum(out_grad, axis=0, dtype=F32),
    ])
    row_sums = jnp.sum(grad_rows, axis=0, dtype=F32)
    vector = jnp.concatenate([sum_all(vector, "col", cols), row_sums, up_bias_part])
    vector = sum_all(sum_all(vector, "row", rows), "dp", dps)
    grads = [vector[i * width : (i + 1) * width] for i in range(6)]
    tail = vector[6 * width :]

    return (
        result[:real],
        inputs_grad[:real],
        grads[0],
        grads[1],
        qkv_sum[:, :head_cols],
        tail[:head_cols],
        qkv_sum[:, head_cols : 2 * head_cols],
        qkv_sum[:, 2 * head_cols :],
        tail[2 * head_cols : 3 * head_cols],
        out_sum.T,
        grads[4],
        grads[2],
        grads[3],
        mlp_sum[:, :hidden_cols],
        tail[3 * head_cols :],
        mlp_sum[:, hidden_cols:].T,
        grads[5],
    )


def solution(mesh):
    stream = P(("dp", "row", "col"), None)
    inward, outward = P("row", "col"), P("col", "row")
    return jax.shard_map(
        functools.partial(
            per_device, mesh.shape["col"], mesh.shape["row"], mesh.shape["dp"]
        ),
        mesh=mesh,
        in_specs=(
            stream, P(), P(), inward, P("col"), inward, inward, P("col"), outward, P(), P(), P(),
            inward, P("col"), outward, P(), stream,
        ),
        out_specs=(
            stream, stream, P(), P(), inward, P("col"), inward, inward, P("col"), outward, P(),
            P(), P(), inward, P("col"), outward, P(),
        ),
        check_vma=False,
    )
```

```python
import functools

import jax
import jax.numpy as jnp
from jax import lax
from jax.experimental import pallas as pl
from jax.experimental.pallas import tpu as pltpu
from jax.sharding import PartitionSpec as P

HEAD_DIM = 64
LENGTH = 1500
LOG2E = 1.4426950408889634
SCALE = HEAD_DIM**-0.5
BLOCK = 256
F32 = jnp.float32
BF16 = jnp.bfloat16


def dims(left_dim, right_dim):
    return (((left_dim,), (right_dim,)), ((), ()))


def dot(left_side, right_side, left_dim, right_dim):
    return lax.dot_general(
        left_side, right_side, dims(left_dim, right_dim), preferred_element_type=F32
    )


def norm_stats(stream):
    center = jnp.mean(stream, axis=1, keepdims=True)
    second = jnp.mean(stream * stream, axis=1, keepdims=True)
    inverse = lax.rsqrt(second - center * center + 1e-05)
    return (stream - center) * inverse, inverse


def norm_backward(upstream, normed, inverse, scale_row):
    scaled = upstream * scale_row
    back_rows = inverse * (
        scaled
        - jnp.mean(scaled, axis=1, keepdims=True)
        - normed * jnp.mean(scaled * normed, axis=1, keepdims=True)
    )
    return back_rows, jnp.sum(upstream * normed, axis=0), jnp.sum(upstream, axis=0)


def key_bias(keys, block_rows, real_rows):
    at = lax.broadcasted_iota(jnp.int32, (keys, 1), 0)
    return jnp.where(lax.rem(at, block_rows) < real_rows, 0.0, -1e30).astype(F32)


def head_at(kind, heads, head):
    start = (kind * heads + head) * HEAD_DIM
    return slice(start, start + HEAD_DIM)


def forward_kernel(heads, block_rows, real_rows, part_ref, whole_ref, o_ref, lse_ref):
    bias = key_bias(whole_ref.shape[0], block_rows, real_rows)
    for head in range(heads):
        queries = part_ref[:, head_at(0, heads, head)]
        keys = whole_ref[:, head_at(1, heads, head)]
        values = whole_ref[:, head_at(2, heads, head)]
        scores = dot(keys, queries, 1, 1) * (SCALE * LOG2E) + bias
        highest = jnp.max(scores, axis=0, keepdims=True)
        exponent = jnp.exp2(scores - highest)
        summed = jnp.sum(exponent, axis=0, keepdims=True)
        probs = (exponent * (1.0 / summed)).astype(BF16)
        turned = dot(values, probs, 0, 0)
        o_ref[:, head_at(0, heads, head)] = jnp.transpose(turned).astype(BF16)
        lse_ref[head : head + 1, :] = highest + jnp.log2(summed)


def backward_kernel(
    heads, chosen, block_rows, real_rows, part_ref, whole_ref, g_ref, lse_ref, *rest
):
    *earlier, out_ref, dk_sum, dv_sum = rest
    step = pl.program_id(0)

    @pl.when(step == 0)
    def _():
        dk_sum[...] = jnp.zeros_like(dk_sum)
        dv_sum[...] = jnp.zeros_like(dv_sum)
        for ref in earlier:
            out_ref[...] = ref[...]

    bias = key_bias(whole_ref.shape[0], block_rows, real_rows)
    at = pl.ds(pl.multiple_of(step * BLOCK, BLOCK), BLOCK)
    for slot, head in enumerate(chosen):
        queries = part_ref[:, head_at(0, heads, head)]
        keys = whole_ref[:, head_at(1, heads, head)]
        values = whole_ref[:, head_at(2, heads, head)]
        grads = g_ref[:, head_at(0, heads, head)]
        scores = dot(keys, queries, 1, 1) * (SCALE * LOG2E) + bias
        probs = jnp.exp2(scores - lse_ref[head : head + 1, :])
        prob_grad = dot(values, grads, 1, 1)
        inner = jnp.sum(probs * prob_grad, axis=0, keepdims=True)
        score_grad = (probs * (prob_grad - inner)).astype(BF16)
        dv_sum[slot] += dot(probs.astype(BF16), grads, 1, 0)
        dk_sum[slot] += dot(score_grad, queries, 1, 0)
        turned = dot(keys, score_grad, 0, 0)
        out_ref[at, head_at(0, heads, head)] = (jnp.transpose(turned) * SCALE).astype(BF16)

    @pl.when(step == pl.num_programs(0) - 1)
    def _():
        for slot, head in enumerate(chosen):
            out_ref[:, head_at(1, heads, head)] = (dk_sum[slot] * SCALE).astype(BF16)
            out_ref[:, head_at(2, heads, head)] = dv_sum[slot].astype(BF16)


def attention_forward(qkv, first, count, block_rows, real_rows):
    tokens, width = qkv.shape[0], qkv.shape[1] // 3
    heads = width // HEAD_DIM
    start = first // BLOCK
    return pl.pallas_call(
        functools.partial(forward_kernel, heads, block_rows, real_rows),
        grid=(count // BLOCK,),
        in_specs=[
            pl.BlockSpec((BLOCK, 3 * width), lambda i: (i + start, 0)),
            pl.BlockSpec((tokens, 3 * width), lambda i: (0, 0)),
        ],
        out_specs=[
            pl.BlockSpec((BLOCK, width), lambda i: (i, 0)),
            pl.BlockSpec((8, BLOCK), lambda i: (0, i)),
        ],
        out_shape=[
            jax.ShapeDtypeStruct((count, width), BF16),
            jax.ShapeDtypeStruct((8, count), F32),
        ],
        compiler_params=pltpu.CompilerParams(vmem_limit_bytes=40 * 1024 * 1024),
        cost_estimate=pl.CostEstimate(
            flops=16 * count * tokens * width,
            bytes_accessed=8 * tokens * width,
            transcendentals=heads * count * tokens,
        ),
        name="attention_forward",
    )(qkv, qkv)


def attention_backward(qkv, grads, lse, chosen, earlier, block_rows, real_rows):
    tokens, width = grads.shape
    heads = width // HEAD_DIM
    whole = pl.BlockSpec((tokens, 3 * width), lambda i: (0, 0))
    return pl.pallas_call(
        functools.partial(backward_kernel, heads, chosen, block_rows, real_rows),
        grid=(tokens // BLOCK,),
        in_specs=[
            pl.BlockSpec((BLOCK, 3 * width), lambda i: (i, 0)),
            whole,
            pl.BlockSpec((BLOCK, width), lambda i: (i, 0)),
            pl.BlockSpec((8, BLOCK), lambda i: (0, i)),
        ]
        + [whole] * len(earlier),
        out_specs=whole,
        out_shape=jax.ShapeDtypeStruct((tokens, 3 * width), BF16),
        scratch_shapes=[
            pltpu.VMEM((len(chosen), tokens, HEAD_DIM), F32),
            pltpu.VMEM((len(chosen), tokens, HEAD_DIM), F32),
        ],
        compiler_params=pltpu.CompilerParams(vmem_limit_bytes=40 * 1024 * 1024),
        cost_estimate=pl.CostEstimate(
            flops=40 * tokens * tokens * HEAD_DIM * len(chosen),
            bytes_accessed=14 * tokens * width,
            transcendentals=len(chosen) * tokens * tokens,
        ),
        name="attention_backward",
    )(qkv, qkv, grads, lse, *earlier)


def swap(block, axis, size, step):
    return lax.ppermute(block, axis, [(i, i ^ step) for i in range(size)])


def few(size):
    return size <= 8 and size & (size - 1) == 0


def tree(terms):
    while len(terms) > 1:
        terms = [terms[i] + terms[i + 1] for i in range(0, len(terms), 2)]
    return terms[0]


def spread(block, axis, size):
    return [block] + [swap(block, axis, size, j) for j in range(1, size)]


def exchange(blocks, axis, size):
    return [blocks[0]] + [swap(blocks[j], axis, size, j) for j in range(1, size)]


def gather_near(block, axis, size):
    return [swap(block, axis, size, j) for j in range(1, size if size != 4 else 3)]


def gather_far(near, axis, size):
    if size != 4:
        return []
    one, two = near
    half = one.shape[1] // 2
    left = swap(one[:, :half], axis, size, 2)
    right = swap(two[:, half:], axis, size, 1)
    return [left, right]


def gathered(block, near, far):
    blocks = [block, *near]
    if far:
        blocks.append(jnp.concatenate(far, axis=1))
    return jnp.concatenate(blocks, axis=0)


def sum_blocks(make, axis, size):
    sent = {j: swap(make(j).astype(BF16), axis, size, j) for j in reversed(range(1, size))}
    return tree([make(0)] + [sent[j].astype(F32) for j in range(1, size)])


def product_operands(source, weight, held, size):
    rows = lambda j: source[j * held : (j + 1) * held]
    if size != 4:
        return [dot(rows(j), weight, 1, 1).astype(BF16) for j in range(1, size)]
    half = weight.shape[0] // 2
    pair = jnp.concatenate([rows(1), rows(3)], axis=0)
    one = dot(pair, weight[:half], 1, 1).astype(BF16)
    two = dot(source[2 * held :], weight[half:], 1, 1).astype(BF16)
    return [one, two]


def send_near(operands, axis, size):
    return [swap(term, axis, size, j + 1) for j, term in enumerate(operands)]


def send_far(found, source, weight, held, axis, size):
    if size != 4:
        return []
    rows = lambda j: source[j * held : (j + 1) * held]
    half = weight.shape[0] // 2
    one, two = found
    far_left = dot(rows(2), weight[:half], 1, 1) + one[held:].astype(F32)
    far_right = dot(rows(1), weight[half:], 1, 1) + two[held:].astype(F32)
    left_back = swap(far_left.astype(BF16), axis, size, 2)
    right_back = swap(far_right.astype(BF16), axis, size, 1)
    return [left_back, right_back]


def add_products(found, back, source, weight, held):
    own = dot(source[:held], weight, 1, 1)
    if not back:
        return tree([own] + [term.astype(F32) for term in found])
    one, two = found
    near = jnp.concatenate([one[:held], two[:held]], axis=1).astype(F32)
    return own + near + jnp.concatenate(back, axis=1).astype(F32)


def finish_products(found, source, weight, held, axis, size):
    back = send_far(found, source, weight, held, axis, size)
    return add_products(found, back, source, weight, held)


def sum_all(vector, axis, size):
    if few(size):
        return tree(spread(vector, axis, size))
    return lax.psum(vector, axis)


def gather_ordered(block, rows):
    if not few(rows):
        return lax.all_gather(block, "row", axis=0, tiled=True)
    me = lax.axis_index("row")
    found = jnp.stack(spread(block, "row", rows))
    order = [
        lax.dynamic_index_in_dim(found, jnp.bitwise_xor(me, r), 0, False) for r in range(rows)
    ]
    return jnp.concatenate(order, axis=0)


def share_out(first, one, two):
    mine = jnp.where(first, one, two)
    other = jnp.where(first, two, one).astype(BF16)
    return mine + swap(other, "dp", 2, 1).astype(F32)


def bring_back(first, mine):
    theirs = swap(mine, "dp", 2, 1)
    return jnp.where(first, mine, theirs), jnp.where(first, theirs, mine)


def sum_weight(total, rows):
    if few(rows):
        me = lax.axis_index("row")
        view = total.reshape(rows, total.shape[0] // rows, total.shape[1])
        pick = lambda j: lax.dynamic_index_in_dim(view, jnp.bitwise_xor(me, j), 0, False)
        return sum_blocks(pick, "row", rows)
    return lax.psum_scatter(total, "row", scatter_dimension=0, tiled=True)


def per_device(
    cols, rows, dps,
    inputs, first_gain, first_shift, query_weight, query_bias, key_weight, value_weight,
    value_bias, out_weight, out_bias, second_gain, second_shift, up_weight, up_bias,
    down_weight, down_bias, cotangent,
):
    real = inputs.shape[0]
    held = -(-real // 128) * 128
    width = inputs.shape[1]
    head_cols = query_weight.shape[1]
    assert real * cols == LENGTH and cols & (cols - 1) == 0
    fill = ((0, held - real), (0, 0))
    padded = jnp.pad(inputs, fill)
    cotangent = jnp.pad(cotangent, fill)

    def block(array, j):
        return array[j * held : (j + 1) * held]

    def join(blocks):
        return jnp.concatenate(blocks, axis=0)

    assert dps == 2
    tie = lax.optimization_barrier
    first = lax.axis_index("dp") == 0
    hidden_cols = up_weight.shape[1]
    first_normed, first_inverse = norm_stats(padded)
    attn_in = (first_normed * first_gain + first_shift).astype(BF16)
    one = jnp.concatenate([query_weight, key_weight], axis=1)
    two = jnp.concatenate([value_weight, out_weight.T], axis=1)
    near_mine = gather_ordered(jnp.where(first, one, two), rows)
    rest_mine = jnp.where(first, up_weight, down_weight.T)
    near_mine, rest_mine = tie((near_mine, rest_mine))
    query_key, value_out = bring_back(first, near_mine)
    joined = jnp.concatenate([query_key, value_out[:, :head_cols]], axis=1)
    out_turned = value_out[:, head_cols:]
    attn_near = gather_near(attn_in, "col", cols)
    attn_far = gather_far(attn_near, "col", cols)
    attn_near, attn_far, out_turned = tie((attn_near, attn_far, out_turned))
    attn_all = gathered(attn_in, attn_near, attn_far)
    rest_mine = lax.all_gather(rest_mine, "row", axis=0, tiled=True)
    up_full, down_turned = bring_back(first, rest_mine)

    joined_bias = jnp.concatenate([query_bias, jnp.zeros_like(query_bias), value_bias])
    qkv = (dot(attn_all, joined, 1, 0) + joined_bias).astype(BF16)

    out_blocks = spread(out_turned, "col", cols)
    out_grad = cotangent.astype(BF16)
    middle_at = cols // 2 * held
    attended_far, lse_far = attention_forward(
        qkv, middle_at, cols * held - middle_at, held, real
    )
    qkv, out_blocks, out_sent, attended_far = tie((qkv, out_blocks, out_grad, attended_far))
    out_near = gather_near(out_sent, "col", cols)
    attended_near, lse_near = attention_forward(qkv, 0, middle_at, held, real)
    attended_near, out_near, up_full, down_turned = tie(
        (attended_near, out_near, up_full, down_turned)
    )
    out_full = jnp.concatenate(out_blocks, axis=1)
    halves = [block(attended_near, j) for j in range(cols // 2)]
    halves += [block(attended_far, j) for j in range(cols - cols // 2)]
    attended_own = jnp.concatenate(exchange(halves, "col", cols), axis=1)
    lse = jnp.concatenate([lse_near, lse_far], axis=1)

    middle = padded + (dot(attended_own, out_full, 1, 1) + out_bias)
    second_normed, second_inverse = norm_stats(middle)
    mlp_in = (second_normed * second_gain + second_shift).astype(BF16)
    mlp_near = gather_near(mlp_in, "col", cols)
    mlp_far = gather_far(mlp_near, "col", cols)
    mlp_near, mlp_far, out_near = tie((mlp_near, mlp_far, out_near))
    out_far = gather_far(out_near, "col", cols)
    mlp_all = gathered(mlp_in, mlp_near, mlp_far)
    out_all = gathered(out_grad, out_near, out_far)
    pre_act = dot(mlp_all, up_full, 1, 0) + up_bias
    hidden_grad = dot(out_all, down_turned, 1, 0)
    below = 0.5 * (1.0 + lax.erf(pre_act * (0.5**0.5)))
    slope = below + pre_act * (jnp.exp(-0.5 * pre_act * pre_act) * 0.3989422804014327)
    hidden = (pre_act * below).astype(BF16)
    pre_grad = (hidden_grad * slope).astype(BF16)
    sent = product_operands(pre_grad, up_full, held, cols)
    sent, pre_late = tie((sent, pre_grad))
    mlp_found = send_near(sent, "col", cols)
    mlp_back = finish_products(mlp_found, pre_grad, up_full, held, "col", cols)
    up_part = dot(mlp_all, pre_late, 0, 0)
    down_part = dot(out_all, hidden, 0, 0)
    mlp_half = share_out(first, up_part, down_part)
    up_bias_part = jnp.sum(pre_late, axis=0, dtype=F32)
    norm_rows, second_gain_part, second_shift_part = norm_backward(
        mlp_back, second_normed, second_inverse, second_gain
    )
    middle_grad = cotangent + norm_rows
    attn_grad = middle_grad.astype(BF16)
    attended_grad_own = dot(attn_grad, out_full, 1, 0).astype(BF16)
    attended_grad = join(
        exchange(
            [attended_grad_own[:, j * head_cols : (j + 1) * head_cols] for j in range(cols)],
            "col",
            cols,
        )
    )

    down_sent = product_operands(hidden, down_turned, held, cols)
    attended_grad, down_sent, mlp_half, attn_late = tie(
        (attended_grad, down_sent, mlp_half, attn_grad)
    )
    down_found = send_near(down_sent, "col", cols)
    mlp_sum = sum_weight(mlp_half, rows)
    heads = tuple(range(head_cols // HEAD_DIM))
    lead = max(1, len(heads) // 3)
    earlier = [attention_backward(qkv, attended_grad, lse, heads[:lead], [], held, real)]
    earlier, down_found, mlp_sum, attn_late = tie((earlier, down_found, mlp_sum, attn_late))
    down_back = send_far(down_found, hidden, down_turned, held, "col", cols)
    out_part = sum_blocks(
        lambda j: dot(attn_late, attended_own[:, j * head_cols : (j + 1) * head_cols], 0, 0),
        "col",
        cols,
    )
    grad_rows = attention_backward(qkv, attended_grad, lse, heads[lead:], earlier, held, real)
    grad_rows, down_back, out_part = tie((grad_rows, down_back, out_part))

    sent = product_operands(grad_rows, joined, held, cols)
    sent, grad_late, down_back = tie((sent, grad_rows, down_back))
    attn_found = send_near(sent, "col", cols)
    attn_back = finish_products(attn_found, grad_rows, joined, held, "col", cols)
    cut = 2 * head_cols
    near_half = share_out(
        first,
        dot(attn_all, grad_late[:, :cut], 0, 0),
        jnp.concatenate([dot(attn_all, grad_late[:, cut:], 0, 0), out_part], axis=1),
    )
    query_key_sum, value_out_sum = bring_back(first, sum_weight(near_half, rows))
    up_sum, down_sum = bring_back(first, mlp_sum)
    result = middle + (
        add_products(down_found, down_back, hidden, down_turned, held) + down_bias
    )
    norm_rows, first_gain_part, first_shift_part = norm_backward(
        attn_back, first_normed, first_inverse, first_gain
    )
    inputs_grad = middle_grad + norm_rows
    vector = jnp.concatenate([
        first_gain_part,
        first_shift_part,
        second_gain_part,
        second_shift_part,
        jnp.sum(attn_grad, axis=0, dtype=F32),
        jnp.sum(out_grad, axis=0, dtype=F32),
    ])
    row_sums = jnp.sum(grad_late, axis=0, dtype=F32)
    vector = jnp.concatenate([sum_all(vector, "col", cols), row_sums, up_bias_part])
    vector = sum_all(sum_all(vector, "row", rows), "dp", dps)
    grads = [vector[i * width : (i + 1) * width] for i in range(6)]
    tail = vector[6 * width :]

    return (
        result[:real],
        inputs_grad[:real],
        grads[0],
        grads[1],
        query_key_sum[:, :head_cols],
        tail[:head_cols],
        query_key_sum[:, head_cols:],
        value_out_sum[:, :head_cols],
        tail[2 * head_cols : 3 * head_cols],
        value_out_sum[:, head_cols:].T,
        grads[4],
        grads[2],
        grads[3],
        up_sum,
        tail[3 * head_cols :],
        down_sum.T,
        grads[5],
    )


def solution(mesh):
    stream = P(("dp", "row", "col"), None)
    inward, outward = P("row", "col"), P("col", "row")
    return jax.shard_map(
        functools.partial(
            per_device, mesh.shape["col"], mesh.shape["row"], mesh.shape["dp"]
        ),
        mesh=mesh,
        in_specs=(
            stream, P(), P(), inward, P("col"), inward, inward, P("col"), outward, P(), P(), P(),
            inward, P("col"), outward, P(), stream,
        ),
        out_specs=(
            stream, stream, P(), P(), inward, P("col"), inward, inward, P("col"), outward, P(),
            P(), P(), inward, P("col"), outward, P(),
        ),
        check_vma=False,
    )
```

```python
import functools

import jax
import jax.numpy as jnp
from jax import lax
from jax.experimental import pallas as pl
from jax.experimental.pallas import tpu as pltpu
from jax.sharding import PartitionSpec as P

HEAD_DIM = 64
LENGTH = 1500
LOG2E = 1.4426950408889634
SCALE = HEAD_DIM**-0.5
BLOCK = 256
F32 = jnp.float32
BF16 = jnp.bfloat16


def dims(left_dim, right_dim):
    return (((left_dim,), (right_dim,)), ((), ()))


def dot(left_side, right_side, left_dim, right_dim):
    return lax.dot_general(
        left_side, right_side, dims(left_dim, right_dim), preferred_element_type=F32
    )


def norm_stats(stream):
    center = jnp.mean(stream, axis=1, keepdims=True)
    second = jnp.mean(stream * stream, axis=1, keepdims=True)
    inverse = lax.rsqrt(second - center * center + 1e-05)
    return (stream - center) * inverse, inverse


def norm_backward(upstream, normed, inverse, scale_row):
    scaled = upstream * scale_row
    back_rows = inverse * (
        scaled
        - jnp.mean(scaled, axis=1, keepdims=True)
        - normed * jnp.mean(scaled * normed, axis=1, keepdims=True)
    )
    return back_rows, jnp.sum(upstream * normed, axis=0), jnp.sum(upstream, axis=0)


def key_bias(keys, block_rows, real_rows):
    at = lax.broadcasted_iota(jnp.int32, (keys, 1), 0)
    return jnp.where(lax.rem(at, block_rows) < real_rows, 0.0, -1e30).astype(F32)


def head_at(kind, heads, head):
    start = (kind * heads + head) * HEAD_DIM
    return slice(start, start + HEAD_DIM)


def forward_kernel(heads, block_rows, real_rows, part_ref, whole_ref, o_ref, lse_ref):
    bias = key_bias(whole_ref.shape[0], block_rows, real_rows)
    for head in range(heads):
        queries = part_ref[:, head_at(0, heads, head)]
        keys = whole_ref[:, head_at(1, heads, head)]
        values = whole_ref[:, head_at(2, heads, head)]
        scores = dot(keys, queries, 1, 1) * (SCALE * LOG2E) + bias
        highest = jnp.max(scores, axis=0, keepdims=True)
        exponent = jnp.exp2(scores - highest)
        summed = jnp.sum(exponent, axis=0, keepdims=True)
        probs = (exponent * (1.0 / summed)).astype(BF16)
        turned = dot(values, probs, 0, 0)
        o_ref[:, head_at(0, heads, head)] = jnp.transpose(turned).astype(BF16)
        lse_ref[head : head + 1, :] = highest + jnp.log2(summed)


def backward_kernel(
    heads, chosen, block_rows, real_rows, part_ref, whole_ref, g_ref, lse_ref, *rest
):
    *earlier, out_ref, dk_sum, dv_sum = rest
    step = pl.program_id(0)

    @pl.when(step == 0)
    def _():
        dk_sum[...] = jnp.zeros_like(dk_sum)
        dv_sum[...] = jnp.zeros_like(dv_sum)
        for ref in earlier:
            out_ref[...] = ref[...]

    bias = key_bias(whole_ref.shape[0], block_rows, real_rows)
    at = pl.ds(pl.multiple_of(step * BLOCK, BLOCK), BLOCK)
    for slot, head in enumerate(chosen):
        queries = part_ref[:, head_at(0, heads, head)]
        keys = whole_ref[:, head_at(1, heads, head)]
        values = whole_ref[:, head_at(2, heads, head)]
        grads = g_ref[:, head_at(0, heads, head)]
        scores = dot(keys, queries, 1, 1) * (SCALE * LOG2E) + bias
        probs = jnp.exp2(scores - lse_ref[head : head + 1, :])
        prob_grad = dot(values, grads, 1, 1)
        inner = jnp.sum(probs * prob_grad, axis=0, keepdims=True)
        score_grad = (probs * (prob_grad - inner)).astype(BF16)
        dv_sum[slot] += dot(probs.astype(BF16), grads, 1, 0)
        dk_sum[slot] += dot(score_grad, queries, 1, 0)
        turned = dot(keys, score_grad, 0, 0)
        out_ref[at, head_at(0, heads, head)] = (jnp.transpose(turned) * SCALE).astype(BF16)

    @pl.when(step == pl.num_programs(0) - 1)
    def _():
        for slot, head in enumerate(chosen):
            out_ref[:, head_at(1, heads, head)] = (dk_sum[slot] * SCALE).astype(BF16)
            out_ref[:, head_at(2, heads, head)] = dv_sum[slot].astype(BF16)


def attention_forward(qkv, first, count, block_rows, real_rows):
    tokens, width = qkv.shape[0], qkv.shape[1] // 3
    heads = width // HEAD_DIM
    start = first // BLOCK
    return pl.pallas_call(
        functools.partial(forward_kernel, heads, block_rows, real_rows),
        grid=(count // BLOCK,),
        in_specs=[
            pl.BlockSpec((BLOCK, 3 * width), lambda i: (i + start, 0)),
            pl.BlockSpec((tokens, 3 * width), lambda i: (0, 0)),
        ],
        out_specs=[
            pl.BlockSpec((BLOCK, width), lambda i: (i, 0)),
            pl.BlockSpec((8, BLOCK), lambda i: (0, i)),
        ],
        out_shape=[
            jax.ShapeDtypeStruct((count, width), BF16),
            jax.ShapeDtypeStruct((8, count), F32),
        ],
        compiler_params=pltpu.CompilerParams(vmem_limit_bytes=40 * 1024 * 1024),
        cost_estimate=pl.CostEstimate(
            flops=16 * count * tokens * width,
            bytes_accessed=8 * tokens * width,
            transcendentals=heads * count * tokens,
        ),
        name="attention_forward",
    )(qkv, qkv)


def attention_backward(qkv, grads, lse, chosen, earlier, block_rows, real_rows):
    tokens, width = grads.shape
    heads = width // HEAD_DIM
    whole = pl.BlockSpec((tokens, 3 * width), lambda i: (0, 0))
    return pl.pallas_call(
        functools.partial(backward_kernel, heads, chosen, block_rows, real_rows),
        grid=(tokens // BLOCK,),
        in_specs=[
            pl.BlockSpec((BLOCK, 3 * width), lambda i: (i, 0)),
            whole,
            pl.BlockSpec((BLOCK, width), lambda i: (i, 0)),
            pl.BlockSpec((8, BLOCK), lambda i: (0, i)),
        ]
        + [whole] * len(earlier),
        out_specs=whole,
        out_shape=jax.ShapeDtypeStruct((tokens, 3 * width), BF16),
        scratch_shapes=[
            pltpu.VMEM((len(chosen), tokens, HEAD_DIM), F32),
            pltpu.VMEM((len(chosen), tokens, HEAD_DIM), F32),
        ],
        compiler_params=pltpu.CompilerParams(vmem_limit_bytes=40 * 1024 * 1024),
        cost_estimate=pl.CostEstimate(
            flops=40 * tokens * tokens * HEAD_DIM * len(chosen),
            bytes_accessed=14 * tokens * width,
            transcendentals=len(chosen) * tokens * tokens,
        ),
        name="attention_backward",
    )(qkv, qkv, grads, lse, *earlier)


def swap(block, axis, size, step):
    return lax.ppermute(block, axis, [(i, i ^ step) for i in range(size)])


def few(size):
    return size <= 8 and size & (size - 1) == 0


def tree(terms):
    while len(terms) > 1:
        terms = [terms[i] + terms[i + 1] for i in range(0, len(terms), 2)]
    return terms[0]


def spread(block, axis, size):
    return [block] + [swap(block, axis, size, j) for j in range(1, size)]


def exchange(blocks, axis, size):
    return [blocks[0]] + [swap(blocks[j], axis, size, j) for j in range(1, size)]


def gather_near(block, axis, size):
    return [swap(block, axis, size, j) for j in range(1, size if size != 4 else 3)]


def gather_far(near, axis, size):
    if size != 4:
        return []
    one, two = near
    half = one.shape[1] // 2
    left = swap(one[:, :half], axis, size, 2)
    right = swap(two[:, half:], axis, size, 1)
    return [left, right]


def gathered(block, near, far):
    blocks = [block, *near]
    if far:
        blocks.append(jnp.concatenate(far, axis=1))
    return jnp.concatenate(blocks, axis=0)


def sum_blocks(make, axis, size):
    sent = {j: swap(make(j).astype(BF16), axis, size, j) for j in reversed(range(1, size))}
    return tree([make(0)] + [sent[j].astype(F32) for j in range(1, size)])


def product_operands(source, weight, held, size):
    rows = lambda j: source[j * held : (j + 1) * held]
    if size != 4:
        return [dot(rows(j), weight, 1, 1).astype(BF16) for j in range(1, size)]
    half = weight.shape[0] // 2
    pair = jnp.concatenate([rows(1), rows(3)], axis=0)
    one = dot(pair, weight[:half], 1, 1).astype(BF16)
    two = dot(source[2 * held :], weight[half:], 1, 1).astype(BF16)
    return [one, two]


def send_near(operands, axis, size):
    return [swap(term, axis, size, j + 1) for j, term in enumerate(operands)]


def send_far(found, source, weight, held, axis, size):
    if size != 4:
        return []
    rows = lambda j: source[j * held : (j + 1) * held]
    half = weight.shape[0] // 2
    one, two = found
    far_left = dot(rows(2), weight[:half], 1, 1) + one[held:].astype(F32)
    far_right = dot(rows(1), weight[half:], 1, 1) + two[held:].astype(F32)
    left_back = swap(far_left.astype(BF16), axis, size, 2)
    right_back = swap(far_right.astype(BF16), axis, size, 1)
    return [left_back, right_back]


def add_products(found, back, source, weight, held):
    own = dot(source[:held], weight, 1, 1)
    if not back:
        return tree([own] + [term.astype(F32) for term in found])
    one, two = found
    near = jnp.concatenate([one[:held], two[:held]], axis=1).astype(F32)
    return own + near + jnp.concatenate(back, axis=1).astype(F32)


def finish_products(found, source, weight, held, axis, size):
    back = send_far(found, source, weight, held, axis, size)
    return add_products(found, back, source, weight, held)


def sum_all(vector, axis, size):
    if few(size):
        return tree(spread(vector, axis, size))
    return lax.psum(vector, axis)


def gather_ordered(block, rows):
    if not few(rows):
        return lax.all_gather(block, "row", axis=0, tiled=True)
    me = lax.axis_index("row")
    found = jnp.stack(spread(block, "row", rows))
    order = [
        lax.dynamic_index_in_dim(found, jnp.bitwise_xor(me, r), 0, False) for r in range(rows)
    ]
    return jnp.concatenate(order, axis=0)


def share_out(first, one, two):
    mine = jnp.where(first, one, two)
    other = jnp.where(first, two, one).astype(BF16)
    return mine + swap(other, "dp", 2, 1).astype(F32)


def bring_back(first, mine):
    theirs = swap(mine, "dp", 2, 1)
    return jnp.where(first, mine, theirs), jnp.where(first, theirs, mine)


def sum_weight(total, rows):
    if few(rows):
        me = lax.axis_index("row")
        view = total.reshape(rows, total.shape[0] // rows, total.shape[1])
        pick = lambda j: lax.dynamic_index_in_dim(view, jnp.bitwise_xor(me, j), 0, False)
        return sum_blocks(pick, "row", rows)
    return lax.psum_scatter(total, "row", scatter_dimension=0, tiled=True)


def per_device(
    cols, rows, dps,
    inputs, first_gain, first_shift, query_weight, query_bias, key_weight, value_weight,
    value_bias, out_weight, out_bias, second_gain, second_shift, up_weight, up_bias,
    down_weight, down_bias, cotangent,
):
    real = inputs.shape[0]
    held = -(-real // 128) * 128
    width = inputs.shape[1]
    head_cols = query_weight.shape[1]
    assert real * cols == LENGTH and cols & (cols - 1) == 0
    fill = ((0, held - real), (0, 0))
    padded = jnp.pad(inputs, fill)
    cotangent = jnp.pad(cotangent, fill)

    def block(array, j):
        return array[j * held : (j + 1) * held]

    def join(blocks):
        return jnp.concatenate(blocks, axis=0)

    assert dps == 2
    tie = lax.optimization_barrier
    first = lax.axis_index("dp") == 0
    hidden_cols = up_weight.shape[1]
    first_normed, first_inverse = norm_stats(padded)
    attn_in = (first_normed * first_gain + first_shift).astype(BF16)
    one = jnp.concatenate([query_weight, key_weight], axis=1)
    two = jnp.concatenate([value_weight, out_weight.T], axis=1)
    attn_in, near_mine = tie((attn_in, jnp.where(first, one, two)))
    near_mine = gather_ordered(near_mine, rows)
    rest_mine = jnp.where(first, up_weight, down_weight.T)
    attn_near = gather_near(attn_in, "col", cols)
    near_mine, rest_mine, attn_near = tie((near_mine, rest_mine, attn_near))
    query_key, value_out = bring_back(first, near_mine)
    joined = jnp.concatenate([query_key, value_out[:, :head_cols]], axis=1)
    out_turned = value_out[:, head_cols:]
    attn_far = gather_far(attn_near, "col", cols)
    attn_near, attn_far, out_turned = tie((attn_near, attn_far, out_turned))
    attn_all = gathered(attn_in, attn_near, attn_far)
    rest_mine = lax.all_gather(rest_mine, "row", axis=0, tiled=True)
    up_full, down_turned = bring_back(first, rest_mine)

    joined_bias = jnp.concatenate([query_bias, jnp.zeros_like(query_bias), value_bias])
    qkv = (dot(attn_all, joined, 1, 0) + joined_bias).astype(BF16)

    out_blocks = spread(out_turned, "col", cols)
    out_grad = cotangent.astype(BF16)
    middle_at = cols // 2 * held
    attended_far, lse_far = attention_forward(
        qkv, middle_at, cols * held - middle_at, held, real
    )
    qkv, out_blocks, out_sent, attended_far = tie((qkv, out_blocks, out_grad, attended_far))
    out_near = gather_near(out_sent, "col", cols)
    attended_near, lse_near = attention_forward(qkv, 0, middle_at, held, real)
    attended_near, out_near, up_full, down_turned = tie(
        (attended_near, out_near, up_full, down_turned)
    )
    out_full = jnp.concatenate(out_blocks, axis=1)
    halves = [block(attended_near, j) for j in range(cols // 2)]
    halves += [block(attended_far, j) for j in range(cols - cols // 2)]
    attended_own = jnp.concatenate(exchange(halves, "col", cols), axis=1)
    lse = jnp.concatenate([lse_near, lse_far], axis=1)

    middle = padded + (dot(attended_own, out_full, 1, 1) + out_bias)
    second_normed, second_inverse = norm_stats(middle)
    mlp_in = (second_normed * second_gain + second_shift).astype(BF16)
    mlp_near = gather_near(mlp_in, "col", cols)
    mlp_far = gather_far(mlp_near, "col", cols)
    mlp_near, mlp_far, out_near = tie((mlp_near, mlp_far, out_near))
    out_far = gather_far(out_near, "col", cols)
    mlp_all = gathered(mlp_in, mlp_near, mlp_far)
    out_all = gathered(out_grad, out_near, out_far)
    pre_act = dot(mlp_all, up_full, 1, 0) + up_bias
    hidden_grad = dot(out_all, down_turned, 1, 0)
    below = 0.5 * (1.0 + lax.erf(pre_act * (0.5**0.5)))
    slope = below + pre_act * (jnp.exp(-0.5 * pre_act * pre_act) * 0.3989422804014327)
    hidden = (pre_act * below).astype(BF16)
    pre_grad = (hidden_grad * slope).astype(BF16)
    sent = product_operands(pre_grad, up_full, held, cols)
    sent, pre_late = tie((sent, pre_grad))
    mlp_found = send_near(sent, "col", cols)
    mlp_back = finish_products(mlp_found, pre_grad, up_full, held, "col", cols)
    up_part = dot(mlp_all, pre_late, 0, 0)
    down_part = dot(out_all, hidden, 0, 0)
    mlp_half = share_out(first, up_part, down_part)
    up_bias_part = jnp.sum(pre_late, axis=0, dtype=F32)
    norm_rows, second_gain_part, second_shift_part = norm_backward(
        mlp_back, second_normed, second_inverse, second_gain
    )
    middle_grad = cotangent + norm_rows
    attn_grad = middle_grad.astype(BF16)
    attended_grad_own = dot(attn_grad, out_full, 1, 0).astype(BF16)
    attended_grad = join(
        exchange(
            [attended_grad_own[:, j * head_cols : (j + 1) * head_cols] for j in range(cols)],
            "col",
            cols,
        )
    )

    down_sent = product_operands(hidden, down_turned, held, cols)
    attended_grad, down_sent, mlp_half, attn_late = tie(
        (attended_grad, down_sent, mlp_half, attn_grad)
    )
    down_found = send_near(down_sent, "col", cols)
    mlp_sum = sum_weight(mlp_half, rows)
    heads = tuple(range(head_cols // HEAD_DIM))
    lead = max(1, len(heads) // 3)
    earlier = [attention_backward(qkv, attended_grad, lse, heads[:lead], [], held, real)]
    earlier, down_found, mlp_sum, attn_late = tie((earlier, down_found, mlp_sum, attn_late))
    down_back = send_far(down_found, hidden, down_turned, held, "col", cols)
    out_part = sum_blocks(
        lambda j: dot(attn_late, attended_own[:, j * head_cols : (j + 1) * head_cols], 0, 0),
        "col",
        cols,
    )
    grad_rows = attention_backward(qkv, attended_grad, lse, heads[lead:], earlier, held, real)
    grad_rows, down_back, out_part = tie((grad_rows, down_back, out_part))

    sent = product_operands(grad_rows, joined, held, cols)
    sent, grad_late, down_back = tie((sent, grad_rows, down_back))
    attn_found = send_near(sent, "col", cols)
    attn_back = finish_products(attn_found, grad_rows, joined, held, "col", cols)
    cut = 2 * head_cols
    near_half = share_out(
        first,
        dot(attn_all, grad_late[:, :cut], 0, 0),
        jnp.concatenate([dot(attn_all, grad_late[:, cut:], 0, 0), out_part], axis=1),
    )
    query_key_sum, value_out_sum = bring_back(first, sum_weight(near_half, rows))
    up_sum, down_sum = bring_back(first, mlp_sum)
    result = middle + (
        add_products(down_found, down_back, hidden, down_turned, held) + down_bias
    )
    norm_rows, first_gain_part, first_shift_part = norm_backward(
        attn_back, first_normed, first_inverse, first_gain
    )
    inputs_grad = middle_grad + norm_rows
    vector = jnp.concatenate([
        first_gain_part,
        first_shift_part,
        second_gain_part,
        second_shift_part,
        jnp.sum(attn_grad, axis=0, dtype=F32),
        jnp.sum(out_grad, axis=0, dtype=F32),
    ])
    row_sums = jnp.sum(grad_late, axis=0, dtype=F32)
    vector = jnp.concatenate([sum_all(vector, "col", cols), row_sums, up_bias_part])
    vector = sum_all(sum_all(vector, "row", rows), "dp", dps)
    grads = [vector[i * width : (i + 1) * width] for i in range(6)]
    tail = vector[6 * width :]

    return (
        result[:real],
        inputs_grad[:real],
        grads[0],
        grads[1],
        query_key_sum[:, :head_cols],
        tail[:head_cols],
        query_key_sum[:, head_cols:],
        value_out_sum[:, :head_cols],
        tail[2 * head_cols : 3 * head_cols],
        value_out_sum[:, head_cols:].T,
        grads[4],
        grads[2],
        grads[3],
        up_sum,
        tail[3 * head_cols :],
        down_sum.T,
        grads[5],
    )


def solution(mesh):
    stream = P(("dp", "row", "col"), None)
    inward, outward = P("row", "col"), P("col", "row")
    return jax.shard_map(
        functools.partial(
            per_device, mesh.shape["col"], mesh.shape["row"], mesh.shape["dp"]
        ),
        mesh=mesh,
        in_specs=(
            stream, P(), P(), inward, P("col"), inward, inward, P("col"), outward, P(), P(), P(),
            inward, P("col"), outward, P(), stream,
        ),
        out_specs=(
            stream, stream, P(), P(), inward, P("col"), inward, inward, P("col"), outward, P(),
            P(), P(), inward, P("col"), outward, P(),
        ),
        check_vma=False,
    )
```
